32 devices in a mesh: uly: 8 (over z, y), blk: 4 (over x, core).
Axes of the slice: x: 2, y: 2, z: 4, core: 2. Of those that a mesh axis runs over, the one named last changes fastest.
Arguments:
- queries: bfloat16 [4096, 1024], P(('blk', 'uly')), may hold values from -6 to 6
- keys: bfloat16 [4096, 1024], P(('blk', 'uly')), may hold values from -6 to 6
- values: bfloat16 [4096, 1024], P(('blk', 'uly')), may hold values from -6 to 6
- lengths: int32 [16], replicated, may hold values from 1 to 512, 4096 in all
- conv_weight: float32 [31, 1024], P(None, 'uly'), may hold values from -8 to 8
- norm_gain: float32 [1024], P('uly'), may hold values from 0.1 to 1.9
- cotangent: bfloat16 [1024, 4096], P('uly', 'blk'), may hold values from -6 to 6
Outputs:
- conv_out: bfloat16 [1024, 4096], P('uly', 'blk')
- grad_queries: bfloat16 [1024, 4096], P('uly', 'blk')
- grad_keys: bfloat16 [1024, 4096], P('uly', 'blk')
- grad_values: bfloat16 [1024, 4096], P('uly', 'blk')
The draws below stay inside these ranges and needn't reach their ends.
Inputs may be any that keep to these rules, and one draw needn't show every extreme that they name: `lengths`: utterances follow one another and cover the 4096 frames; one utterance has exactly 512 frames.
All inputs are finite; a program needn't handle non-finite values.
Results may differ from the reference program's by a relative error of at most 0.03.
Values may be sent and summed in bfloat16 or wider, within the bound.
No kernel may reach another device: no remote copies, remote signals or barrier semaphores. Data moves between devices by JAX's collectives and lax.ppermute only.
A program may use at most 64 MiB of HBM per device.

```python
import math
import jax
import jax.numpy as jnp
import numpy as np
from jax import lax

D = 1024
HEADS = 16
KERNEL = 31
HEAD_DIM = 64
MAXLEN = 512
FRAMES = 4096
UTTS = 16
QB = 512
HALF = 15


def drawn_pair(key):
    shape_full = (FRAMES, D)
    query_noise = jax.random.normal(jax.random.fold_in(key, 11), shape_full, jnp.float32)
    key_noise = jax.random.normal(jax.random.fold_in(key, 12), shape_full, jnp.float32)
    return (jnp.clip(query_noise, -6.0, 6.0), jnp.clip(key_noise, -6.0, 6.0))


def draw_queries(key, part):
    return drawn_pair(key)[0].astype(jnp.bfloat16)


def draw_keys(key, part):
    return drawn_pair(key)[1].astype(jnp.bfloat16)


def draw_conv_weight(key, part):
    base_taps = jax.random.normal(jax.random.fold_in(key, 21), (KERNEL, D), jnp.float32)
    channel_level = jnp.exp(jax.random.uniform(jax.random.fold_in(key, 22), (1, D), jnp.float32, 0.0, 2.3026))
    return jnp.clip(base_taps, -4.0, 4.0) * channel_level * KERNEL ** (-0.5)


def level_of(own_key, dims, shards, smallest, largest):
    def one(axis_at, shards_of):
        heights = jax.random.uniform(jax.random.fold_in(jax.random.fold_in(own_key, 6), axis_at), (shards_of,), jnp.float32, smallest / len(shards), largest / len(shards))
        return jnp.repeat(jnp.exp(heights), dims[axis_at] // shards_of).reshape((-1,) + (1,) * (len(dims) - axis_at - 1))

    gain = one(*shards[0])
    for cut in shards[1:]:
        gain = gain * one(*cut)
    return gain


def length_profile(amount, total, limit, slope):
    loads = [(1 << 20) // math.isqrt(standing ** slope) + 1 for standing in range(2, amount + 1)]
    spare, given = total - limit - (amount - 1), [1] * (amount - 1)
    while spare > 0:
        free = [i for i in range(amount - 1) if given[i] < limit]
        whole, left = sum([loads[i] for i in free]), spare
        for i in free:
            extra = min(limit - given[i], max(1, left * loads[i] // whole), spare)
            given[i] = given[i] + extra
            spare = spare - extra
    return np.array([limit] + given)


def uneven(rng, number_of, total, bound, lean):
    if number_of == 2:
        one = jax.random.randint(rng, (), max(1, total - bound), min(bound, total - 1) + 1)
        return jnp.stack([one, total - one])
    sizes = jnp.asarray(length_profile(number_of, total, bound, lean), jnp.int32)
    twos = (number_of - 1) // 2
    giver, taker = sizes[1:1 + 2 * twos:2], sizes[2:2 + 2 * twos:2]
    room = jnp.minimum(giver - 1, bound - taker)
    shifted = jax.random.randint(jax.random.fold_in(rng, 1), (twos,), 0, 1 << 20) % (room + 1)
    sizes = sizes.at[1:1 + 2 * twos:2].set(giver - shifted).at[2:2 + 2 * twos:2].set(taker + shifted)
    return sizes[jax.random.permutation(jax.random.fold_in(rng, 2), number_of)]


def noise(stream_key, shape, scale, limit, pieces=(), kind=jnp.bfloat16):
    loudness = level_of(stream_key, shape, pieces, -0.22, 0.18) if pieces else 1.0
    drawn = jax.random.normal(stream_key, shape, jnp.float32) * scale * loudness
    return jnp.minimum(jnp.maximum(drawn, -limit), limit).astype(kind)


def setup_inputs(seed: int = 0) -> dict:
    key_of = jax.random.split(jax.random.key(seed), 8)
    return {
        "queries": draw_queries(jax.random.fold_in(key_of[7], 71), 0),
        "keys": draw_keys(jax.random.fold_in(key_of[7], 71), 0),
        "values": noise(key_of[2], (FRAMES, D), 1.0, 6.0, ((0, 32),)),
        "lengths": uneven(key_of[3], UTTS, FRAMES, MAXLEN, 2).astype(jnp.int32),
        "conv_weight": draw_conv_weight(jax.random.fold_in(key_of[7], 71), 0),
        "norm_gain": jnp.clip(1.0 + 0.18 * jax.random.normal(key_of[5], (D,), jnp.float32), 0.1, 1.9),
        "cotangent": noise(key_of[6], (D, FRAMES), 1.0, 6.0, ((0, 8), (1, 4))),
    }


def segment_ids(lengths, frames, frame_total):
    starts = (jnp.cumsum(lengths) - lengths).astype(jnp.int32)
    seg_ids = lax.optimization_barrier(jnp.sum((starts[None, :] <= frames[:, None]).astype(jnp.int32), axis=1)) - 1
    inside = (frames >= 0) & (frames < frame_total)
    return jnp.where(inside, seg_ids, -1).astype(jnp.int32)

def rounded(values_in):
    return lax.optimization_barrier(values_in.astype(jnp.bfloat16)).astype(jnp.float32)

def tile_probs(query_rows, key_rows, query_seg, key_seg):
    scores = HEAD_DIM ** (-0.5) * jnp.einsum('rhe,she->hrs', query_rows.astype(jnp.float32), key_rows.astype(jnp.float32))
    same_seg = (query_seg[:, None] == key_seg[None, :])[None]
    row_top = lax.optimization_barrier(jnp.max(jnp.where(same_seg, scores, -1e+30), axis=2, keepdims=True))
    shifted_exp = jnp.where(same_seg, jnp.exp(scores - row_top), 0.0)
    row_total = lax.optimization_barrier(jnp.sum(shifted_exp, axis=2, keepdims=True))
    return shifted_exp / row_total

def reference(queries, keys, values, lengths, conv_weight, norm_gain, cotangent):
    score_scale = HEAD_DIM ** (-0.5)
    window = QB + 2 * MAXLEN
    shape_heads = (FRAMES, HEADS, HEAD_DIM)
    q_heads = queries.reshape(shape_heads)
    pad_rows = ((MAXLEN, MAXLEN), (0, 0), (0, 0))
    k_pad = jnp.pad(keys.reshape(shape_heads), pad_rows)
    v_pad = jnp.pad(values.reshape(shape_heads), pad_rows)
    seg_own = segment_ids(lengths, jnp.arange(FRAMES, dtype=jnp.int32), FRAMES)
    seg_pad = segment_ids(lengths, jnp.arange(FRAMES + 2 * MAXLEN, dtype=jnp.int32) - MAXLEN, FRAMES)
    seg_conv = segment_ids(lengths, jnp.arange(FRAMES + 2 * HALF, dtype=jnp.int32) - HALF, FRAMES)
    starts = jnp.arange(FRAMES // QB, dtype=jnp.int32) * QB

    def window_rows(row_start):
        return (lax.dynamic_slice_in_dim(q_heads, row_start, QB, 0), lax.dynamic_slice_in_dim(k_pad, row_start, window, 0), lax.dynamic_slice_in_dim(v_pad, row_start, window, 0), lax.dynamic_slice_in_dim(seg_own, row_start, QB, 0), lax.dynamic_slice_in_dim(seg_pad, row_start, window, 0))

    def forward_block(row_start):
        query_rows, key_rows, value_rows, query_seg, key_seg = window_rows(row_start)
        probs = tile_probs(query_rows, key_rows, query_seg, key_seg)
        attended = jnp.einsum('hrs,she->rhe', rounded(probs), value_rows.astype(jnp.float32))
        return attended.astype(jnp.bfloat16)
    attended = lax.map(forward_block, starts).reshape(FRAMES, D)
    attended_pad = jnp.pad(attended.astype(jnp.float32), ((HALF, HALF), (0, 0)))
    conv_sum = jnp.zeros((FRAMES, D), jnp.float32)
    for tap_index in range(KERNEL):
        same_seg = (seg_conv[tap_index:tap_index + FRAMES] == seg_own)[:, None]
        conv_sum = conv_sum + conv_weight[tap_index][None, :] * jnp.where(same_seg, attended_pad[tap_index:tap_index + FRAMES], 0.0)
    grouped = conv_sum.reshape(shape_heads)
    spread = jnp.sqrt(lax.optimization_barrier(jnp.mean(grouped * grouped, axis=2, keepdims=True)) + 1e-05)
    normed = grouped / spread
    pre_act = normed.reshape(FRAMES, D) * norm_gain[None, :]
    sigmoid_gate = jax.nn.sigmoid(pre_act)
    conv_out = (pre_act * sigmoid_gate).astype(jnp.bfloat16)
    grad_pre = cotangent.astype(jnp.float32).T * sigmoid_gate * (1.0 + pre_act * (1.0 - sigmoid_gate))
    weighted = (grad_pre * norm_gain[None, :]).reshape(shape_heads)
    grad_conv = ((weighted - normed * lax.optimization_barrier(jnp.mean(weighted * normed, axis=2, keepdims=True))) / spread).reshape(FRAMES, D)
    grad_pad = jnp.pad(grad_conv, ((HALF, HALF), (0, 0)))
    grad_sum = jnp.zeros((FRAMES, D), jnp.float32)
    for tap_index in range(KERNEL):
        offset = 2 * HALF - tap_index
        same_seg = (seg_conv[offset:offset + FRAMES] == seg_own)[:, None]
        grad_sum = grad_sum + conv_weight[tap_index][None, :] * jnp.where(same_seg, grad_pad[offset:offset + FRAMES], 0.0)
    grad_attended = grad_sum.astype(jnp.bfloat16)
    row_delta = lax.optimization_barrier(jnp.sum((grad_attended.astype(jnp.float32) * attended.astype(jnp.float32)).reshape(shape_heads), axis=2))
    grad_heads = grad_attended.reshape(shape_heads)

    def backward_block(running, row_start):
        grad_k, grad_v = running
        query_rows, key_rows, value_rows, query_seg, key_seg = window_rows(row_start)
        grad_rows = lax.dynamic_slice_in_dim(grad_heads, row_start, QB, 0).astype(jnp.float32)
        delta_rows = lax.dynamic_slice_in_dim(row_delta, row_start, QB, 0)
        probs = tile_probs(query_rows, key_rows, query_seg, key_seg)
        grad_p = jnp.einsum('rhe,she->hrs', grad_rows, value_rows.astype(jnp.float32))
        grad_s = rounded(probs * (grad_p - delta_rows.T[:, :, None]))
        grad_q = score_scale * jnp.einsum('hrs,she->rhe', grad_s, key_rows.astype(jnp.float32))
        key_term = score_scale * jnp.einsum('hrs,rhe->she', grad_s, query_rows.astype(jnp.float32))
        value_term = jnp.einsum('hrs,rhe->she', rounded(probs), grad_rows)
        grad_k = lax.dynamic_update_slice_in_dim(grad_k, lax.dynamic_slice_in_dim(grad_k, row_start, window, 0) + key_term, row_start, 0)
        grad_v = lax.dynamic_update_slice_in_dim(grad_v, lax.dynamic_slice_in_dim(grad_v, row_start, window, 0) + value_term, row_start, 0)
        return ((grad_k, grad_v), grad_q.astype(jnp.bfloat16))
    zero_pad = jnp.zeros((FRAMES + 2 * MAXLEN, HEADS, HEAD_DIM), jnp.float32)
    (grad_k, grad_v), grad_q = lax.scan(backward_block, (zero_pad, zero_pad), starts)
    grad_queries = grad_q.reshape(FRAMES, D)
    grad_keys = grad_k[MAXLEN:MAXLEN + FRAMES].reshape(FRAMES, D).astype(jnp.bfloat16)
    grad_values = grad_v[MAXLEN:MAXLEN + FRAMES].reshape(FRAMES, D).astype(jnp.bfloat16)
    return (conv_out.T, grad_queries.T, grad_keys.T, grad_values.T)
```

```python
import functools

import jax
import jax.numpy as jnp
from jax import lax
from jax.experimental import pallas as pl
from jax.experimental.pallas import tpu as pltpu
from jax.sharding import PartitionSpec as P

KERNEL = 31
HEAD_DIM = 64
HALF = KERNEL // 2
LANES = 128
GAP = 16
F32 = jnp.float32
BF16 = jnp.bfloat16


def dot_nt(a, b):
    return lax.dot_general(a, b, (((1,), (1,)), ((), ())), preferred_element_type=F32)


def dot_nn(a, b):
    return lax.dot_general(a, b, (((1,), (0,)), ((), ())), preferred_element_type=F32)


def widened(rows):
    if rows.shape[1] == LANES:
        return rows
    return jnp.concatenate([rows, jnp.zeros_like(rows)], axis=1)


def head_mean(x, ones_twice):
    top = x.astype(BF16)
    rest = (x - top.astype(F32)).astype(BF16)
    return dot_nn(jnp.concatenate([top, rest], axis=1), ones_twice)


def kernel(
    dims, place_ref, lengths_ref, own_ref, near_ref, far_ref, cot_ref, cot_lo_ref, cot_hi_ref,
    taps_ref, gain_ref, out_ref, dq_ref, dk_ref, dv_ref,
    qx, kx, vx, cx, ox, dqx, dkx, dvx, weights, grad_s, att_pad, grad_pad, att, rinv, lhs, num, den,
):
    heads, block, maxlen, piece, peers, utts, step = dims
    half = peers // 2
    me, first_frame = place_ref[0], place_ref[1]

    for d in range(peers):
        u = me ^ d
        row = pl.multiple_of(maxlen + u * piece, piece)
        for i, dst in enumerate((qx, kx, vx)):
            dst[pl.ds(row, piece), :] = widened(own_ref[d, i].astype(F32))
        side = pl.multiple_of(
            jnp.where(u < half, maxlen + block + u * piece, (u - half) * piece), piece
        )
        src = near_ref if d < half else far_ref
        for i, dst in enumerate((qx, kx, vx)):
            dst[pl.ds(side, piece), :] = widened(src[d % half, i].astype(F32))
    for ref, base in ((cot_lo_ref, 0), (cot_ref, maxlen), (cot_hi_ref, maxlen + block)):
        for at in range(0, ref.shape[1], 128):
            cx[base + at : base + at + 128, :] = widened(ref[:, at : at + 128].astype(F32).T)

    lane = lax.broadcasted_iota(jnp.int32, (1, LANES), 1)
    low = lane < HEAD_DIM
    ones_twice = jnp.where(
        lax.broadcasted_iota(jnp.int32, (2 * LANES, LANES), 0) % LANES // HEAD_DIM
        == lax.broadcasted_iota(jnp.int32, (2 * LANES, LANES), 1) // HEAD_DIM,
        1.0 / HEAD_DIM,
        0.0,
    ).astype(BF16)
    gain = gain_ref[...]

    def utterance(start, length, width):
        mine = [low, jnp.logical_not(low)][:heads]
        rows = pl.ds(start, width)
        chunk = 128
        valid = lax.broadcasted_iota(jnp.int32, (width, 1), 0) < length
        key_bias = jnp.where(
            lax.broadcasted_iota(jnp.int32, (1, width), 1) < length, 0.0, -1e30
        )
        q = qx[rows, :] * HEAD_DIM ** (-0.5)
        k = kx[rows, :].astype(BF16)
        v = vx[rows, :]
        v_ones = [jnp.where(m, v, 1.0).astype(BF16) for m in mine]
        q_own = [jnp.where(m, q, 0.0).astype(BF16) for m in mine]

        for at in range(0, width, chunk):
            part = pl.ds(at, chunk)
            accs = []
            for h in range(heads):
                scores = dot_nt(q_own[h][at : at + chunk], k) + key_bias
                top = jnp.max(scores, axis=1, keepdims=True)
                e = jnp.exp(scores - top).astype(BF16)
                weights[h, part, :width] = e
                accs.append(dot_nn(e, v_ones[h]))
            if heads == 1:
                accs.append(jnp.ones_like(accs[0]))
            total = pltpu.roll(jnp.where(low, accs[1], accs[0]), HEAD_DIM, 1)
            inverse = 1.0 / total
            rinv[part, :] = inverse
            attended = (jnp.where(low, accs[0], accs[1]) * inverse).astype(BF16).astype(F32)
            att_pad[pl.ds(GAP + at, chunk), :] = jnp.where(
                valid[at : at + chunk], attended, 0.0
            )
        att_pad[pl.ds(0, GAP), :] = jnp.zeros((GAP, LANES), F32)
        att_pad[pl.ds(GAP + width, GAP), :] = jnp.zeros((GAP, LANES), F32)
        grad_pad[pl.ds(0, GAP), :] = jnp.zeros((GAP, LANES), F32)
        grad_pad[pl.ds(GAP + width, GAP), :] = jnp.zeros((GAP, LANES), F32)

        conv_chunk = 64
        for at in range(0, width, conv_chunk):
            conv = jnp.zeros((conv_chunk, LANES), F32)
            for j in range(KERNEL):
                conv = conv + taps_ref[j : j + 1, :] * att_pad[
                    pl.ds(at + GAP - HALF + j, conv_chunk), :
                ]
            inv_spread = lax.rsqrt(head_mean(conv * conv, ones_twice) + 1e-05)
            normed = conv * inv_spread
            pre_act = normed * gain
            gate = 1.0 / (1.0 + jnp.exp(-pre_act))
            ox[pl.ds(start + at, conv_chunk), :] = pre_act * gate
            grad_pre = cx[pl.ds(start + at, conv_chunk), :] * gate * (1.0 + pre_act * (1.0 - gate))
            weighted = grad_pre * gain
            grad_conv = (weighted - normed * head_mean(weighted * normed, ones_twice)) * inv_spread
            grad_pad[pl.ds(GAP + at, conv_chunk), :] = jnp.where(
                valid[at : at + conv_chunk], grad_conv, 0.0
            )
        for at in range(0, width, conv_chunk):
            part = pl.ds(at, conv_chunk)
            total = jnp.zeros((conv_chunk, LANES), F32)
            for j in range(KERNEL):
                total = total + taps_ref[j : j + 1, :] * grad_pad[
                    pl.ds(at + GAP + HALF - j, conv_chunk), :
                ]
            total = jnp.where(valid[at : at + conv_chunk], total, 0.0).astype(BF16).astype(F32)
            att[part, :] = total * rinv[part, :]

        grads = att[pl.ds(0, width), :]
        cross = pltpu.roll(-grads * att_pad[pl.ds(GAP, width), :], HEAD_DIM, 1)
        left = [jnp.where(m, grads, cross).astype(BF16) for m in mine]
        for at in range(0, width, chunk):
            part = pl.ds(at, chunk)
            outs = []
            for h in range(heads):
                moved = dot_nt(left[h][at : at + chunk], v_ones[h])
                ds = (weights[h, part, :width].astype(F32) * moved).astype(BF16)
                grad_s[h, part, :width] = ds
                outs.append(dot_nn(ds, k))
            dq = outs[0] if heads == 1 else jnp.where(low, outs[0], outs[1])
            dqx[pl.ds(start + at, chunk), :] = dq * HEAD_DIM ** (-0.5)
        q_t = q.T.astype(BF16)
        grads_t = grads.T.astype(BF16)
        for lhs_t, rhs, dst in ((q_t, grad_s, dkx), (grads_t, weights, dvx)):
            terms = [
                dot_nn(lhs_t[h * HEAD_DIM : (h + 1) * HEAD_DIM], rhs[h, :width, :width])
                for h in range(heads)
            ]
            if heads == 1:
                terms.append(jnp.zeros_like(terms[0]))
            dst[rows, :] = jnp.concatenate(terms, axis=0).T

    def visit(i, start):
        length = lengths_ref[i]

        @pl.when((start < maxlen + block) & (start + length > maxlen))
        def _():
            for width in range(step, maxlen + 1, step):

                @pl.when((length <= width) & (length > width - step))
                def _():
                    utterance(start, length, width)

        return start + length

    lax.fori_loop(0, utts, visit, maxlen - first_frame)

    channels = heads * HEAD_DIM
    for src, dst in ((ox, out_ref), (dqx, dq_ref), (dkx, dk_ref), (dvx, dv_ref)):
        for at in range(0, block, 128):
            tile = src[maxlen + at : maxlen + at + 128, :].T
            dst[:, at : at + 128] = tile[:channels].astype(BF16)


def on_device(queries, keys, values, lengths, conv_weight, norm_gain, cotangent):
    peers, blocks = lax.axis_size("uly"), lax.axis_size("blk")
    me, blk = lax.axis_index("uly"), lax.axis_index("blk")
    piece = queries.shape[0]
    channels = queries.shape[1] // peers
    heads = channels // HEAD_DIM
    block = cotangent.shape[1]
    maxlen = block // 2
    half = peers // 2
    utts = lengths.shape[0]

    up = [(i, i + 1) for i in range(blocks - 1)]
    down = [(i + 1, i) for i in range(blocks - 1)]
    cot_lo = lax.ppermute(cotangent[:, block - maxlen :], "blk", up)
    cot_hi = lax.ppermute(cotangent[:, :maxlen], "blk", down)

    packed = jnp.stack(
        [x.reshape(piece, peers, channels).transpose(1, 0, 2) for x in (queries, keys, values)],
        axis=1,
    )
    pieces = []
    for d in range(peers):
        own = lax.dynamic_index_in_dim(packed, me ^ d, 0, keepdims=False)
        if d:
            own = lax.ppermute(own, "uly", [(i, i ^ d) for i in range(peers)])
        pieces.append(own)

    def to_neighbour(group, is_near):
        route = []
        for b in range(blocks):
            for u in range(peers):
                to = b - 1 if (u < half) == is_near else b + 1
                if 0 <= to < blocks:
                    route.append((u * blocks + b, u * blocks + to))
        return lax.ppermute(group, ("uly", "blk"), route)

    near = jnp.stack(pieces[:half])
    far = jnp.stack(pieces[half:])
    near_halo = to_neighbour(near, True)
    far_halo = to_neighbour(far, False)
    own = jnp.concatenate([near, far], axis=0)

    taps, gain = conv_weight, norm_gain[None, :]
    if channels < LANES:
        taps = jnp.pad(taps, ((0, 0), (0, LANES - channels)))
        gain = jnp.pad(gain, ((0, 0), (0, LANES - channels)))
    place = jnp.stack([me, blk * block]).astype(jnp.int32)
    rows = block + 2 * maxlen
    dims = (heads, block, maxlen, piece, peers, utts, maxlen // 4)
    smem = pl.BlockSpec(memory_space=pltpu.SMEM)
    vmem = pl.BlockSpec(memory_space=pltpu.VMEM)
    out = jax.ShapeDtypeStruct((channels, block), BF16)
    return pl.pallas_call(
        functools.partial(kernel, dims),
        out_shape=(out,) * 4,
        in_specs=[smem, smem] + [vmem] * 8,
        out_specs=(vmem,) * 4,
        scratch_shapes=[pltpu.VMEM((rows, LANES), F32)] * 8
        + [pltpu.VMEM((heads, maxlen, maxlen), BF16)] * 2
        + [pltpu.VMEM((maxlen + 2 * GAP, LANES), F32)] * 2
        + [pltpu.VMEM((maxlen, LANES), F32)] * 5,
        compiler_params=pltpu.CompilerParams(vmem_limit_bytes=48 * 2**20),
        name="segments",
    )(place, lengths, own, near_halo, far_halo, cotangent, cot_lo, cot_hi, taps, gain)


def solution(mesh):
    in_specs = (
        P(("blk", "uly"), None),
        P(("blk", "uly"), None),
        P(("blk", "uly"), None),
        P(),
        P(None, "uly"),
        P("uly"),
        P("uly", "blk"),
    )
    out_specs = (P("uly", "blk"), P("uly", "blk"), P("uly", "blk"), P("uly", "blk"))
    return jax.shard_map(
        on_device, mesh=mesh, in_specs=in_specs, out_specs=out_specs, check_vma=False
    )
```

```python
import functools

import jax
import jax.numpy as jnp
from jax import lax
from jax.experimental import pallas as pl
from jax.experimental.pallas import tpu as pltpu
from jax.sharding import PartitionSpec as P

KERNEL = 31
HEAD_DIM = 64
HALF = KERNEL // 2
LANES = 128
GAP = 16
F32 = jnp.float32
BF16 = jnp.bfloat16


def dot_nt(a, b):
    return lax.dot_general(a, b, (((1,), (1,)), ((), ())), preferred_element_type=F32)


def dot_nn(a, b):
    return lax.dot_general(a, b, (((1,), (0,)), ((), ())), preferred_element_type=F32)


def widened(rows):
    if rows.shape[1] == LANES:
        return rows
    return jnp.concatenate([rows, jnp.zeros_like(rows)], axis=1)


def head_mean(x, ones_twice):
    top = x.astype(BF16)
    rest = (x - top.astype(F32)).astype(BF16)
    return dot_nn(jnp.concatenate([top, rest], axis=1), ones_twice)


def pack_kernel(dims, q_ref, k_ref, v_ref, cot_ref, *outs):
    channels, block, maxlen, piece, peers = dims
    me = lax.axis_index("uly")
    low = me < peers // 2
    near_ref, far_ref = outs[0], outs[1]
    for d in range(peers - 1, -1, -1):
        for i, src in enumerate((q_ref, k_ref, v_ref)):
            if channels % LANES == 0:
                at = pl.ds(pl.multiple_of((me ^ d) * channels, channels), channels)
                tile = src[:, at]
            else:
                tile = src[me ^ d]
            outs[2 + d][i] = tile
    for j in range(maxlen // piece):
        first = cot_ref[:, j * piece : (j + 1) * piece].astype(F32).T.astype(BF16)
        second = cot_ref[:, block - maxlen + j * piece : block - maxlen + (j + 1) * piece]
        second = second.astype(F32).T.astype(BF16)
        near_ref[j] = jnp.where(low, first, second)
        far_ref[j] = jnp.where(low, second, first)


def kernel(dims, edges, lengths_ref, taps_ref, gain_ref, cot_ref, *refs):
    heads, block, maxlen, piece, peers, utts, step = dims
    half = peers // 2
    channels = heads * HEAD_DIM
    own_refs, refs = refs[:peers], refs[peers:]
    if edges:
        (near_in, far_in, *before), refs = refs[:6], refs[6:]
    outs = refs[:4]
    (
        qx, kx, vx, cx, ox, dqx, dkx, dvx, weights, grad_s, att_pad, grad_pad, att, rinv, scores,
    ) = refs[4:]
    me, first_frame = lax.axis_index("uly"), lax.axis_index("blk") * block
    base = maxlen if edges else 0

    def side_row(u, at):
        return pl.multiple_of(jnp.where(u < half, maxlen + block + at, at), piece)

    for d in range(peers):
        u = me ^ d
        row = pl.multiple_of(base + u * piece, piece)
        for i, dst in enumerate((qx, kx, vx)):
            dst[pl.ds(row, piece), :] = widened(own_refs[d][i].astype(F32))
        if edges:
            halo, at = (near_in if d < half else far_in), 3 * (d % half)
            side = side_row(u, jnp.where(u < half, u, u - half) * piece)
            for i, dst in enumerate((qx, kx, vx)):
                dst[pl.ds(side, piece), :] = widened(halo[at + i].astype(F32))
    for at in range(0, block, 128):
        tile = cot_ref[:, at : at + 128].astype(F32).T
        cx[base + at : base + at + 128, :] = widened(tile)
    if edges:
        for j in range(maxlen // piece):
            for side, src in ((me, near_in), (me ^ half, far_in)):
                tile = src[3 * half + j].astype(F32)
                cx[pl.ds(side_row(side, j * piece), piece), :] = widened(tile)
    else:
        for ref in (qx, kx, vx, cx):
            ref[block : block + maxlen, :] = jnp.zeros((maxlen, LANES), F32)

    lane = lax.broadcasted_iota(jnp.int32, (1, LANES), 1)
    low = lane < HEAD_DIM
    ones_twice = jnp.where(
        lax.broadcasted_iota(jnp.int32, (2 * LANES, LANES), 0) % LANES // HEAD_DIM
        == lax.broadcasted_iota(jnp.int32, (2 * LANES, LANES), 1) // HEAD_DIM,
        1.0 / HEAD_DIM,
        0.0,
    ).astype(BF16)
    gain = gain_ref[...]

    def utterance(start, length, width):
        mine = [low, jnp.logical_not(low)][:heads]
        rows = pl.ds(start, width)
        soft = 64
        valid = lax.broadcasted_iota(jnp.int32, (width, 1), 0) < length
        key_bias = jnp.where(
            lax.broadcasted_iota(jnp.int32, (1, width), 1) < length, 0.0, -1e30
        )
        q = qx[rows, :] * HEAD_DIM ** (-0.5)
        k = kx[rows, :].astype(BF16)
        v = vx[rows, :]
        v_ones = [jnp.where(m, v, 1.0).astype(BF16) for m in mine]
        q_own = [jnp.where(m, q, 0.0).astype(BF16) for m in mine]

        for h in range(heads):
            scores[h, :width, :width] = dot_nt(q_own[h], k)
        for h in range(heads):
            for at in range(0, width, soft):
                part = pl.ds(at, soft)
                tile = scores[h, part, :width] + key_bias
                top = jnp.max(tile, axis=1, keepdims=True)
                weights[h, part, :width] = jnp.exp(tile - top).astype(BF16)
        accs = [dot_nn(weights[h, :width, :width], v_ones[h]) for h in range(heads)]
        if heads == 1:
            accs.append(jnp.ones_like(accs[0]))
        total = pltpu.roll(jnp.where(low, accs[1], accs[0]), HEAD_DIM, 1)
        inverse = 1.0 / total
        rinv[pl.ds(0, width), :] = inverse
        attended = (jnp.where(low, accs[0], accs[1]) * inverse).astype(BF16).astype(F32)
        att_pad[pl.ds(GAP, width), :] = jnp.where(valid, attended, 0.0)
        att_pad[pl.ds(0, GAP), :] = jnp.zeros((GAP, LANES), F32)
        att_pad[pl.ds(GAP + width, GAP), :] = jnp.zeros((GAP, LANES), F32)
        grad_pad[pl.ds(0, GAP), :] = jnp.zeros((GAP, LANES), F32)
        grad_pad[pl.ds(GAP + width, GAP), :] = jnp.zeros((GAP, LANES), F32)

        conv_chunk = 64
        for at in range(0, width, conv_chunk):
            conv = jnp.zeros((conv_chunk, LANES), F32)
            for j in range(KERNEL):
                conv = conv + taps_ref[j : j + 1, :] * att_pad[
                    pl.ds(at + GAP - HALF + j, conv_chunk), :
                ]
            inv_spread = lax.rsqrt(head_mean(conv * conv, ones_twice) + 1e-05)
            normed = conv * inv_spread
            pre_act = normed * gain
            gate = 1.0 / (1.0 + jnp.exp(-pre_act))
            ox[pl.ds(start + at, conv_chunk), :] = pre_act * gate
            grad_pre = cx[pl.ds(start + at, conv_chunk), :] * gate * (1.0 + pre_act * (1.0 - gate))
            weighted = grad_pre * gain
            grad_conv = (weighted - normed * head_mean(weighted * normed, ones_twice)) * inv_spread
            grad_pad[pl.ds(GAP + at, conv_chunk), :] = jnp.where(
                valid[at : at + conv_chunk], grad_conv, 0.0
            )
        for at in range(0, width, conv_chunk):
            part = pl.ds(at, conv_chunk)
            total = jnp.zeros((conv_chunk, LANES), F32)
            for j in range(KERNEL):
                total = total + taps_ref[j : j + 1, :] * grad_pad[
                    pl.ds(at + GAP + HALF - j, conv_chunk), :
                ]
            total = jnp.where(valid[at : at + conv_chunk], total, 0.0).astype(BF16).astype(F32)
            att[part, :] = total * rinv[part, :]

        grads = att[pl.ds(0, width), :]
        cross = pltpu.roll(-grads * att_pad[pl.ds(GAP, width), :], HEAD_DIM, 1)
        left = [jnp.where(m, grads, cross).astype(BF16) for m in mine]
        for h in range(heads):
            scores[h, :width, :width] = dot_nt(left[h], v_ones[h])
        for h in range(heads):
            for at in range(0, width, soft):
                part = pl.ds(at, soft)
                ds = weights[h, part, :width].astype(F32) * scores[h, part, :width]
                grad_s[h, part, :width] = ds.astype(BF16)
        outs = [dot_nn(grad_s[h, :width, :width], k) for h in range(heads)]
        dq = outs[0] if heads == 1 else jnp.where(low, outs[0], outs[1])
        dqx[rows, :] = dq * HEAD_DIM ** (-0.5)
        q_t = q.T.astype(BF16)
        grads_t = grads.T.astype(BF16)
        for lhs_t, rhs, dst in ((q_t, grad_s, dkx), (grads_t, weights, dvx)):
            terms = [
                dot_nn(lhs_t[h * HEAD_DIM : (h + 1) * HEAD_DIM], rhs[h, :width, :width])
                for h in range(heads)
            ]
            if heads == 1:
                terms.append(jnp.zeros_like(terms[0]))
            dst[rows, :] = jnp.concatenate(terms, axis=0).T

    def visit(i, carry):
        start, head, tail = carry
        length = lengths_ref[i]
        end = start + length
        at_head = (start < 0) & (end > 0)
        at_tail = (start < block) & (end > block)

        @pl.when((at_head | at_tail) if edges else ((start >= 0) & (end <= block)))
        def _():
            for width in range(step, maxlen + 1, step):

                @pl.when((length <= width) & (length > width - step))
                def _():
                    utterance(base + start, length, width)

        return end, jnp.where(at_head, end, head), jnp.where(at_tail, start, tail)

    _, head, tail = lax.fori_loop(0, utts, visit, (-first_frame, 0, block))

    frame = lax.broadcasted_iota(jnp.int32, (1, 128), 1)
    for i, src in enumerate((ox, dqx, dkx, dvx)):
        for at in range(0, block, 128):
            tile = src[base + at : base + at + 128, :].T[:channels].astype(BF16)
            if edges:
                crossing = (frame + at < head) | (frame + at >= tail)
                tile = jnp.where(crossing, tile, before[i][:, at : at + 128])
            outs[i][:, at : at + 128] = tile


def on_device(queries, keys, values, lengths, conv_weight, norm_gain, cotangent):
    peers, blocks = lax.axis_size("uly"), lax.axis_size("blk")
    piece = queries.shape[0]
    channels = queries.shape[1] // peers
    heads = channels // HEAD_DIM
    block = cotangent.shape[1]
    maxlen = block // 2
    half = peers // 2
    utts = lengths.shape[0]

    smem = pl.BlockSpec(memory_space=pltpu.SMEM)
    vmem = pl.BlockSpec(memory_space=pltpu.VMEM)

    def shaped(count):
        return jax.ShapeDtypeStruct((count, piece, channels), BF16)

    sources = (queries, keys, values)
    if channels % LANES:
        sources = tuple(x.reshape(piece, peers, channels).transpose(1, 0, 2) for x in sources)
    near, far, *parts = pl.pallas_call(
        functools.partial(pack_kernel, (channels, block, maxlen, piece, peers)),
        out_shape=(shaped(maxlen // piece),) * 2 + (shaped(3),) * peers,
        in_specs=[vmem] * 4,
        out_specs=(vmem,) * (2 + peers),
        name="pack",
    )(*sources, cotangent)

    def to_neighbour(x, from_half):
        route = []
        for u in range(peers):
            for b in range(blocks):
                to = b - 1 if (u < half) == (from_half == 0) else b + 1
                if 0 <= to < blocks:
                    route.append((u * blocks + b, u * blocks + to))
        return lax.ppermute(x, ("uly", "blk"), route)

    own = parts[:1] + [None] * (peers - 1)
    order = sorted(range(1, peers), key=lambda d: d)
    for d in order:
        own[d] = lax.ppermute(parts[d], "uly", [(i, i ^ d) for i in range(peers)])
    near_group = jnp.concatenate(own[:half] + [near], axis=0)
    near_in = to_neighbour(near_group, 0)
    far_in = to_neighbour(jnp.concatenate(own[half:] + [far], axis=0), 1)

    taps, gain = conv_weight, norm_gain[None, :]
    if channels < LANES:
        taps = jnp.pad(taps, ((0, 0), (0, LANES - channels)))
        gain = jnp.pad(gain, ((0, 0), (0, LANES - channels)))
    dims = (heads, block, maxlen, piece, peers, utts, maxlen // 4)
    out = jax.ShapeDtypeStruct((channels, block), BF16)

    def call(edges, *arrays):
        rows = block + (2 if edges else 1) * maxlen
        return pl.pallas_call(
            functools.partial(kernel, dims, edges),
            out_shape=(out,) * 4,
            in_specs=[smem] + [vmem] * len(arrays),
            out_specs=(vmem,) * 4,
            scratch_shapes=[pltpu.VMEM((rows, LANES), F32)] * 8
            + [pltpu.VMEM((heads, maxlen, maxlen), BF16)] * 2
            + [pltpu.VMEM((maxlen + 2 * GAP, LANES), F32)] * 2
            + [pltpu.VMEM((maxlen, LANES), F32)] * 2
            + [pltpu.VMEM((heads, maxlen, maxlen), F32)],
            compiler_params=pltpu.CompilerParams(vmem_limit_bytes=40 * 2**20),
            cost_estimate=pl.CostEstimate(
                flops=24 * heads * block * maxlen * HEAD_DIM,
                bytes_accessed=16 * block * channels,
                transcendentals=heads * block * maxlen,
            ),
            name="edges" if edges else "inner",
        )(lengths, *arrays)

    inner = call(False, taps, gain, cotangent, *own)
    return call(True, taps, gain, cotangent, *own, near_in, far_in, *inner)


def solution(mesh):
    in_specs = (
        P(("blk", "uly"), None),
        P(("blk", "uly"), None),
        P(("blk", "uly"), None),
        P(),
        P(None, "uly"),
        P("uly"),
        P("uly", "blk"),
    )
    out_specs = (P("uly", "blk"), P("uly", "blk"), P("uly", "blk"), P("uly", "blk"))
    return jax.shard_map(
        on_device, mesh=mesh, in_specs=in_specs, out_specs=out_specs, check_vma=False
    )
```

```python
import functools

import jax
import jax.numpy as jnp
from jax import lax
from jax.experimental import pallas as pl
from jax.experimental.pallas import tpu as pltpu
from jax.sharding import PartitionSpec as P

KERNEL = 31
HEAD_DIM = 64
HALF = KERNEL // 2
LANES = 128
GAP = 16
SWEEP = 128
F32 = jnp.float32
BF16 = jnp.bfloat16


def dot_nt(a, b):
    return lax.dot_general(a, b, (((1,), (1,)), ((), ())), preferred_element_type=F32)


def dot_nn(a, b):
    return lax.dot_general(a, b, (((1,), (0,)), ((), ())), preferred_element_type=F32)


def widened(rows):
    if rows.shape[1] == LANES:
        return rows
    return jnp.concatenate([rows, jnp.zeros_like(rows)], axis=1)


def head_mean(x, ones_twice):
    top = x.astype(BF16)
    rest = (x - top.astype(F32)).astype(BF16)
    return dot_nn(jnp.concatenate([top, rest], axis=1), ones_twice)


def pack_kernel(dims, q_ref, k_ref, v_ref, cot_ref, *outs):
    channels, block, maxlen, piece, peers = dims
    me = lax.axis_index("uly")
    low = me < peers // 2
    near_ref, far_ref = outs[0], outs[1]
    for d in range(peers - 1, -1, -1):
        for i, src in enumerate((q_ref, k_ref, v_ref)):
            if channels % LANES == 0:
                at = pl.ds(pl.multiple_of((me ^ d) * channels, channels), channels)
                tile = src[:, at]
            else:
                tile = src[me ^ d]
            outs[2 + d][i] = tile
    for j in range(maxlen // piece):
        first = cot_ref[:, j * piece : (j + 1) * piece].astype(F32).T.astype(BF16)
        second = cot_ref[:, block - maxlen + j * piece : block - maxlen + (j + 1) * piece]
        second = second.astype(F32).T.astype(BF16)
        near_ref[j] = jnp.where(low, first, second)
        far_ref[j] = jnp.where(low, second, first)


def kernel(dims, phase, lengths_ref, taps_ref, gain_ref, cot_ref, *refs):
    heads, block, maxlen, piece, peers, utts, step = dims
    half = peers // 2
    channels = heads * HEAD_DIM
    near, edges = phase == "near", phase == "edges"
    masked = not edges
    count = half if near else peers
    own_refs, refs = refs[:count], refs[count:]
    if edges:
        (near_in, far_in, last_in, *before), refs = refs[:11], refs[11:]
    outs = refs[:4]
    (
        qx, kx, vx, cx, ox, dqx, dkx, dvx, weights, grad_s, att_pad, grad_pad, att, rinv, scores,
        waiting,
    ) = refs[4:]
    me, first_frame = lax.axis_index("uly"), lax.axis_index("blk") * block
    base = maxlen if edges else 0

    def side_row(u, at):
        return pl.multiple_of(jnp.where(u < half, maxlen + block + at, at), piece)

    for d in range(count):
        u = me ^ d
        row = pl.multiple_of(base + u * piece, piece)
        for i, dst in enumerate((qx, kx, vx)):
            dst[pl.ds(row, piece), :] = widened(own_refs[d][i].astype(F32))
        if edges:
            if d < half:
                halo, at = near_in, 3 * d
            elif d < half + half // 2:
                halo, at = far_in, half + 3 * (d - half)
            else:
                halo, at = last_in, 3 * (d - half - half // 2)
            side = side_row(u, jnp.where(u < half, u, u - half) * piece)
            for i, dst in enumerate((qx, kx, vx)):
                dst[pl.ds(side, piece), :] = widened(halo[at + i].astype(F32))
    for at in range(0, block, 128):
        tile = cot_ref[:, at : at + 128].astype(F32).T
        cx[base + at : base + at + 128, :] = widened(tile)
    if edges:
        for j in range(maxlen // piece):
            for side, src, at in ((me, near_in, 3 * half), (me ^ half, far_in, 0)):
                tile = src[at + j].astype(F32)
                cx[pl.ds(side_row(side, j * piece), piece), :] = widened(tile)
    else:
        for ref in (qx, kx, vx, cx):
            ref[block : block + maxlen, :] = jnp.zeros((maxlen, LANES), F32)
    if near:
        rest = pl.ds(pl.multiple_of(jnp.where(me < half, maxlen, 0), maxlen), maxlen)
        for ref in (qx, kx, vx):
            ref[rest, :] = jnp.zeros((maxlen, LANES), F32)

    lane = lax.broadcasted_iota(jnp.int32, (1, LANES), 1)
    low = lane < HEAD_DIM
    ones_twice = jnp.where(
        lax.broadcasted_iota(jnp.int32, (2 * LANES, LANES), 0) % LANES // HEAD_DIM
        == lax.broadcasted_iota(jnp.int32, (2 * LANES, LANES), 1) // HEAD_DIM,
        1.0 / HEAD_DIM,
        0.0,
    ).astype(BF16)
    gain = gain_ref[...]

    mine = [low, jnp.logical_not(low)][:heads]

    def utterances(group, width):
        slots = range(len(group))
        soft, conv_chunk = min(64, width), 64
        rows = [pl.ds(start, width) for start, _ in group]
        index = lax.broadcasted_iota(jnp.int32, (width, 1), 0)
        column = lax.broadcasted_iota(jnp.int32, (1, width), 1)
        valid = [index < length for _, length in group]
        key_bias = [jnp.where(column < length, 0.0, -1e30) for _, length in group]

        def kept(ref, at, count, slot, new):
            place = pl.ds(group[slot][0] + at, count)
            if masked:
                new = jnp.where(valid[slot][at : at + count], new, ref[place, :])
            ref[place, :] = new

        q, k, v_ones, q_own = [], [], [], []
        for i in slots:
            q.append(qx[rows[i], :] * HEAD_DIM ** (-0.5))
            k.append(kx[rows[i], :].astype(BF16))
            v = vx[rows[i], :]
            v_ones.append([jnp.where(m, v, 1.0).astype(BF16) for m in mine])
            q_own.append([jnp.where(m, q[i], 0.0).astype(BF16) for m in mine])

        for i in slots:
            for h in range(heads):
                scores[i, h, :width, :width] = dot_nt(q_own[i][h], k[i])
        for i in slots:
            for h in range(heads):
                for at in range(0, width, soft):
                    part = pl.ds(at, soft)
                    tile = scores[i, h, part, :width] + key_bias[i]
                    top = jnp.max(tile, axis=1, keepdims=True)
                    weights[i, h, part, :width] = jnp.exp(tile - top).astype(BF16)
        for i in slots:
            accs = [dot_nn(weights[i, h, :width, :width], v_ones[i][h]) for h in range(heads)]
            if heads == 1:
                accs.append(jnp.ones_like(accs[0]))
            total = pltpu.roll(jnp.where(low, accs[1], accs[0]), HEAD_DIM, 1)
            inverse = 1.0 / total
            rinv[i, :width, :] = inverse
            attended = (jnp.where(low, accs[0], accs[1]) * inverse).astype(BF16).astype(F32)
            att_pad[i, GAP : GAP + width, :] = jnp.where(valid[i], attended, 0.0)
            for ref in (att_pad, grad_pad):
                ref[i, :GAP, :] = jnp.zeros((GAP, LANES), F32)
                ref[i, GAP + width : 2 * GAP + width, :] = jnp.zeros((GAP, LANES), F32)

        def swept(src, sign):
            def rows_of(c, _):
                at = c * SWEEP
                if not isinstance(c, int):
                    at = pl.multiple_of(at, SWEEP)
                for i in slots:
                    total = jnp.zeros((SWEEP, LANES), F32)
                    for j in range(KERNEL):
                        begin = at + (GAP + sign * (j - HALF))
                        total = total + taps_ref[j : j + 1, :] * src[i, pl.ds(begin, SWEEP), :]
                    att[i, pl.ds(at, SWEEP), :] = total
                return 0

            if width <= SWEEP:
                rows_of(0, 0)
            else:
                lax.fori_loop(0, width // SWEEP, rows_of, 0)

        swept(att_pad, 1)
        for i in slots:
            for at in range(0, width, conv_chunk):
                conv = att[i, at : at + conv_chunk, :]
                inv_spread = lax.rsqrt(head_mean(conv * conv, ones_twice) + 1e-05)
                normed = conv * inv_spread
                pre_act = normed * gain
                gate = 1.0 / (1.0 + jnp.exp(-pre_act))
                kept(ox, at, conv_chunk, i, pre_act * gate)
                upper = cx[pl.ds(group[i][0] + at, conv_chunk), :]
                grad_pre = upper * gate * (1.0 + pre_act * (1.0 - gate))
                weighted = grad_pre * gain
                mean = head_mean(weighted * normed, ones_twice)
                grad_conv = (weighted - normed * mean) * inv_spread
                grad_pad[i, GAP + at : GAP + at + conv_chunk, :] = jnp.where(
                    valid[i][at : at + conv_chunk], grad_conv, 0.0
                )
        swept(grad_pad, -1)
        for i in slots:
            att[i, :width, :] = jnp.where(valid[i], att[i, :width, :], 0.0).astype(BF16).astype(F32)

        grads = [att[i, :width, :] * rinv[i, :width, :] for i in slots]
        for i in slots:
            cross = pltpu.roll(-grads[i] * att_pad[i, GAP : GAP + width, :], HEAD_DIM, 1)
            for h in range(heads):
                left = jnp.where(mine[h], grads[i], cross).astype(BF16)
                scores[i, h, :width, :width] = dot_nt(left, v_ones[i][h])
        for i in slots:
            for h in range(heads):
                for at in range(0, width, soft):
                    part = pl.ds(at, soft)
                    ds = weights[i, h, part, :width].astype(F32) * scores[i, h, part, :width]
                    grad_s[i, h, part, :width] = ds.astype(BF16)
        for i in slots:
            outs = [dot_nn(grad_s[i, h, :width, :width], k[i]) for h in range(heads)]
            dq = outs[0] if heads == 1 else jnp.where(low, outs[0], outs[1])
            kept(dqx, 0, width, i, dq * HEAD_DIM ** (-0.5))
            for lhs, rhs, dst in ((q[i], grad_s, dkx), (grads[i], weights, dvx)):
                lhs_t = lhs.T.astype(BF16)
                terms = [
                    dot_nn(lhs_t[h * HEAD_DIM : (h + 1) * HEAD_DIM], rhs[i, h, :width, :width])
                    for h in range(heads)
                ]
                if heads == 1:
                    terms.append(jnp.zeros_like(terms[0]))
                kept(dst, 0, width, i, jnp.concatenate(terms, axis=0).T)

    first = jnp.where(me < half, 0, maxlen)

    longest_near = maxlen - step

    def single(start, length):
        for width in range(step, (longest_near if near else maxlen) + 1, step):

            @pl.when((length <= width) & (length > width - step))
            def _():
                utterances([(base + start, length)], width)

    def double(start, length, other_start, other_length, widths):
        for width in widths:

            @pl.when((length <= width) & (length > width - step))
            def _():
                utterances([(base + start, length), (base + other_start, other_length)], width)

    def visit(i, carry):
        start, head, tail, low_end, high_end, tail_length, head_length = carry
        length = jnp.where(i < utts, lengths_ref[jnp.minimum(i, utts - 1)], 0)
        end = start + length
        present = length > 0
        at_head = (start < 0) & (end > 0)
        at_tail = present & (start < block) & (end > block)
        at_near = present & (start >= first) & (end <= first + maxlen) & (length <= longest_near)
        inside = present & (start >= 0) & (end <= block) & jnp.logical_not(at_near)
        if near:

            @pl.when(at_near)
            def _():
                single(start, length)

        elif not edges:
            short = 2 * step
            last = i == utts
            kind = jnp.where(length > step, 1, 0)
            upper = jnp.where(last, 1, kind)
            upper_start, upper_length = waiting[0, upper], waiting[1, upper]
            lower_start = jnp.where(last, waiting[0, 0], start)
            lower_length = jnp.where(last, waiting[1, 0], length)
            fits = last | (inside & (length <= short))
            both = fits & (upper_length > 0) & (lower_length > 0)

            @pl.when(fits)
            def _():
                waiting[0, kind] = start
                waiting[1, kind] = jnp.where(both, 0, length)

            @pl.when(both)
            def _():
                double(upper_start, upper_length, lower_start, lower_length, (step, short))

            held = upper_length > 0
            alone = jnp.where(last, jnp.where(held, upper_length, lower_length), length)

            @pl.when((last & jnp.logical_not(both)) | (inside & (length > short)))
            def _():
                single(jnp.where(last & held, upper_start, lower_start), alone)

        return (
            end,
            jnp.where(at_head, end, head),
            jnp.where(at_tail, start, tail),
            jnp.where(at_near, jnp.minimum(low_end, start), low_end),
            jnp.where(at_near, end, high_end),
            jnp.where(at_tail, length, tail_length),
            jnp.where(at_head, length, head_length),
        )

    if not (near or edges):
        waiting[1, 0] = 0
        waiting[1, 1] = 0
    carry = (-first_frame, 0, block, block, 0, 0, 0)
    steps = utts if near or edges else utts + 1
    carry = lax.fori_loop(0, steps, visit, carry)
    _, head, tail, low_end, high_end, tail_length, head_length = carry
    if edges:
        head_start = head - head_length
        most = jnp.maximum(head_length, tail_length)
        together = (most > maxlen - step) & (jnp.minimum(head_length, tail_length) > maxlen // 2)

        @pl.when(together)
        def _():
            utterances([(base + head_start, head_length), (base + tail, tail_length)], maxlen)

        def one(i, _):
            start = jnp.where(i == 0, head_start, tail)
            length = jnp.where(i == 0, head_length, tail_length)
            single(start, jnp.where(together, 0, length))
            return 0

        lax.fori_loop(0, 2, one, 0)

    frame = lax.broadcasted_iota(jnp.int32, (1, 128), 1)
    for i, src in enumerate((ox, dqx, dkx, dvx)):
        for at in range(0, block, 128):
            tile = src[base + at : base + at + 128, :].T[:channels].astype(BF16)
            if edges:
                crossing = (frame + at < head) | (frame + at >= tail)
                in_near = (frame + at >= low_end) & (frame + at < high_end)
                inner = jnp.where(
                    in_near, before[i][:, at : at + 128], before[4 + i][:, at : at + 128]
                )
                tile = jnp.where(crossing, tile, inner)
            outs[i][:, at : at + 128] = tile


def on_device(queries, keys, values, lengths, conv_weight, norm_gain, cotangent):
    peers, blocks = lax.axis_size("uly"), lax.axis_size("blk")
    piece = queries.shape[0]
    channels = queries.shape[1] // peers
    heads = channels // HEAD_DIM
    block = cotangent.shape[1]
    maxlen = block // 2
    half = peers // 2
    utts = lengths.shape[0]

    smem = pl.BlockSpec(memory_space=pltpu.SMEM)
    vmem = pl.BlockSpec(memory_space=pltpu.VMEM)

    def shaped(count):
        return jax.ShapeDtypeStruct((count, piece, channels), BF16)

    sources = (queries, keys, values)
    if channels % LANES:
        sources = tuple(x.reshape(piece, peers, channels).transpose(1, 0, 2) for x in sources)
    near, far, *parts = pl.pallas_call(
        functools.partial(pack_kernel, (channels, block, maxlen, piece, peers)),
        out_shape=(shaped(maxlen // piece),) * 2 + (shaped(3),) * peers,
        in_specs=[vmem] * 4,
        out_specs=(vmem,) * (2 + peers),
        name="pack",
    )(*sources, cotangent)

    def to_neighbour(x, from_half):
        route = []
        for u in range(peers):
            for b in range(blocks):
                to = b - 1 if (u < half) == (from_half == 0) else b + 1
                if 0 <= to < blocks:
                    route.append((u * blocks + b, u * blocks + to))
        return lax.ppermute(x, ("uly", "blk"), route)

    own = parts[:1] + [None] * (peers - 1)
    order = sorted(range(1, peers), key=lambda d: d)
    for d in order:
        own[d] = lax.ppermute(parts[d], "uly", [(i, i ^ d) for i in range(peers)])
    near_group = jnp.concatenate(own[:half] + [near], axis=0)
    taps, gain = conv_weight, norm_gain[None, :]
    if channels < LANES:
        taps = jnp.pad(taps, ((0, 0), (0, LANES - channels)))
        gain = jnp.pad(gain, ((0, 0), (0, LANES - channels)))
    dims = (heads, block, maxlen, piece, peers, utts, maxlen // 4)
    out = jax.ShapeDtypeStruct((channels, block), BF16)

    def call(phase, *arrays):
        rows = block + (2 if phase == "edges" else 1) * maxlen
        held = 32 * rows * LANES + 16 * heads * maxlen * maxlen
        return pl.pallas_call(
            functools.partial(kernel, dims, phase),
            out_shape=(out,) * 4,
            in_specs=[smem] + [vmem] * len(arrays),
            out_specs=(vmem,) * 4,
            scratch_shapes=[pltpu.VMEM((rows, LANES), F32)] * 8
            + [pltpu.VMEM((2, heads, maxlen, maxlen), BF16)] * 2
            + [pltpu.VMEM((2, maxlen + 2 * GAP, LANES), F32)] * 2
            + [pltpu.VMEM((2, maxlen, LANES), F32)] * 2
            + [pltpu.VMEM((2, heads, maxlen, maxlen), F32)]
            + [pltpu.SMEM((2, 2), jnp.int32)],
            compiler_params=pltpu.CompilerParams(vmem_limit_bytes=held + 20 * 2**20),
            cost_estimate=pl.CostEstimate(
                flops=24 * heads * block * maxlen * HEAD_DIM,
                bytes_accessed=16 * block * channels,
                transcendentals=heads * block * maxlen,
            ),
            name=phase,
        )(lengths, *arrays)

    near_in = to_neighbour(near_group, 0)
    first = call("near", taps, gain, cotangent, *own[:half])
    own[half], *first = lax.optimization_barrier((own[half], *first))
    middle = half + half // 2
    far_in = to_neighbour(jnp.concatenate([far] + own[half:middle], axis=0), 1)
    last_in = to_neighbour(jnp.concatenate(own[middle:], axis=0), 1)

    inner = call("inner", taps, gain, cotangent, *own)
    return call("edges", taps, gain, cotangent, *own, near_in, far_in, last_in, *first, *inner)


def solution(mesh):
    in_specs = (
        P(("blk", "uly"), None),
        P(("blk", "uly"), None),
        P(("blk", "uly"), None),
        P(),
        P(None, "uly"),
        P("uly"),
        P("uly", "blk"),
    )
    out_specs = (P("uly", "blk"), P("uly", "blk"), P("uly", "blk"), P("uly", "blk"))
    return jax.shard_map(
        on_device, mesh=mesh, in_specs=in_specs, out_specs=out_specs, check_vma=False
    )
```

```python
import functools

import jax
import jax.numpy as jnp
from jax import lax
from jax.experimental import pallas as pl
from jax.experimental.pallas import tpu as pltpu
from jax.sharding import PartitionSpec as P

KERNEL = 31
HEAD_DIM = 64
HALF = KERNEL // 2
LANES = 128
GAP = 16
PLAN = 8
SWEEP = 128
F32 = jnp.float32
BF16 = jnp.bfloat16


def dot_nt(a, b):
    return lax.dot_general(a, b, (((1,), (1,)), ((), ())), preferred_element_type=F32)


def dot_nn(a, b):
    return lax.dot_general(a, b, (((1,), (0,)), ((), ())), preferred_element_type=F32)


def widened(rows):
    if rows.shape[1] == LANES:
        return rows
    return jnp.concatenate([rows, jnp.zeros_like(rows)], axis=1)


def head_mean(x, ones_twice):
    top = x.astype(BF16)
    rest = (x - top.astype(F32)).astype(BF16)
    return dot_nn(jnp.concatenate([top, rest], axis=1), ones_twice)


def pack_kernel(dims, q_ref, k_ref, v_ref, cot_ref, *outs):
    channels, block, maxlen, piece, peers = dims
    me = lax.axis_index("uly")
    low = me < peers // 2
    near_ref, far_ref = outs[0], outs[1]
    for d in range(peers - 1, -1, -1):
        for i, src in enumerate((q_ref, k_ref, v_ref)):
            if channels % LANES == 0:
                at = pl.ds(pl.multiple_of((me ^ d) * channels, channels), channels)
                tile = src[:, at]
            else:
                tile = src[me ^ d]
            outs[2 + d][i] = tile
    for j in range(maxlen // piece):
        first = cot_ref[:, j * piece : (j + 1) * piece].astype(F32).T.astype(BF16)
        second = cot_ref[:, block - maxlen + j * piece : block - maxlen + (j + 1) * piece]
        second = second.astype(F32).T.astype(BF16)
        near_ref[j] = jnp.where(low, first, second)
        far_ref[j] = jnp.where(low, second, first)


def kernel(dims, phase, lengths_ref, taps_ref, gain_ref, cot_ref, *refs):
    heads, block, maxlen, piece, peers, utts, step = dims
    half = peers // 2
    channels = heads * HEAD_DIM
    near, edges = phase == "near", phase == "edges"
    masked = not edges
    count = half if near else peers
    own_refs, refs = refs[:count], refs[count:]
    if edges:
        (near_in, far_in, *before), refs = refs[:10], refs[10:]
    outs = refs[:4]
    plan_ref = lengths_ref
    if near:
        plan_ref, refs = refs[4], refs[:4] + refs[5:]
    (
        qx, kx, vx, cx, ox, dqx, dkx, dvx, weights, grad_s, att_pad, grad_pad, att, rinv, scores,
        waiting,
    ) = refs[4:]
    me, first_frame = lax.axis_index("uly"), lax.axis_index("blk") * block
    base = maxlen if edges else 0

    def side_row(u, at):
        return pl.multiple_of(jnp.where(u < half, maxlen + block + at, at), piece)

    for d in range(count):
        u = me ^ d
        row = pl.multiple_of(base + u * piece, piece)
        for i, dst in enumerate((qx, kx, vx)):
            dst[pl.ds(row, piece), :] = widened(own_refs[d][i].astype(F32))
        if edges:
            if d < half:
                halo, at = near_in, 3 * d
            else:
                halo, at = far_in, half + 3 * (d - half)
            side = side_row(u, jnp.where(u < half, u, u - half) * piece)
            for i, dst in enumerate((qx, kx, vx)):
                dst[pl.ds(side, piece), :] = widened(halo[at + i].astype(F32))
    for at in range(0, block, 128):
        tile = cot_ref[:, at : at + 128].astype(F32).T
        cx[base + at : base + at + 128, :] = widened(tile)
    if edges:
        for j in range(maxlen // piece):
            for side, src, at in ((me, near_in, 3 * half), (me ^ half, far_in, 0)):
                tile = src[at + j].astype(F32)
                cx[pl.ds(side_row(side, j * piece), piece), :] = widened(tile)
    else:
        for ref in (qx, kx, vx, cx):
            ref[block : block + maxlen, :] = jnp.zeros((maxlen, LANES), F32)
    if near:
        rest = pl.ds(pl.multiple_of(jnp.where(me < half, maxlen, 0), maxlen), maxlen)
        for ref in (qx, kx, vx):
            ref[rest, :] = jnp.zeros((maxlen, LANES), F32)

    lane = lax.broadcasted_iota(jnp.int32, (1, LANES), 1)
    low = lane < HEAD_DIM
    ones_twice = jnp.where(
        lax.broadcasted_iota(jnp.int32, (2 * LANES, LANES), 0) % LANES // HEAD_DIM
        == lax.broadcasted_iota(jnp.int32, (2 * LANES, LANES), 1) // HEAD_DIM,
        1.0 / HEAD_DIM,
        0.0,
    ).astype(BF16)
    gain = gain_ref[...]

    mine = [low, jnp.logical_not(low)][:heads]

    def utterances(group, width):
        slots = range(len(group))
        soft, conv_chunk = min(64, width), 64
        rows = [pl.ds(start, width) for start, _ in group]
        index = lax.broadcasted_iota(jnp.int32, (width, 1), 0)
        column = lax.broadcasted_iota(jnp.int32, (1, width), 1)
        valid = [index < length for _, length in group]
        key_bias = [jnp.where(column < length, 0.0, -1e30) for _, length in group]

        def kept(ref, at, count, slot, new):
            place = pl.ds(group[slot][0] + at, count)
            if masked:
                new = jnp.where(valid[slot][at : at + count], new, ref[place, :])
            ref[place, :] = new

        q, k, v_ones, q_own = [], [], [], []
        for i in slots:
            q.append(qx[rows[i], :] * HEAD_DIM ** (-0.5))
            k.append(kx[rows[i], :].astype(BF16))
            v = vx[rows[i], :]
            v_ones.append([jnp.where(m, v, 1.0).astype(BF16) for m in mine])
            q_own.append([jnp.where(m, q[i], 0.0).astype(BF16) for m in mine])

        for i in slots:
            for h in range(heads):
                scores[i, h, :width, :width] = dot_nt(q_own[i][h], k[i])
        for i in slots:
            for h in range(heads):
                for at in range(0, width, soft):
                    part = pl.ds(at, soft)
                    tile = scores[i, h, part, :width] + key_bias[i]
                    top = jnp.max(tile, axis=1, keepdims=True)
                    weights[i, h, part, :width] = jnp.exp(tile - top).astype(BF16)
        for i in slots:
            accs = [dot_nn(weights[i, h, :width, :width], v_ones[i][h]) for h in range(heads)]
            if heads == 1:
                accs.append(jnp.ones_like(accs[0]))
            total = pltpu.roll(jnp.where(low, accs[1], accs[0]), HEAD_DIM, 1)
            inverse = 1.0 / total
            rinv[i, :width, :] = inverse
            attended = (jnp.where(low, accs[0], accs[1]) * inverse).astype(BF16).astype(F32)
            att_pad[i, GAP : GAP + width, :] = jnp.where(valid[i], attended, 0.0)
            for ref in (att_pad, grad_pad):
                ref[i, :GAP, :] = jnp.zeros((GAP, LANES), F32)
                ref[i, GAP + width : 2 * GAP + width, :] = jnp.zeros((GAP, LANES), F32)

        def swept(src, sign):
            def rows_of(c, _):
                at = c * SWEEP
                if not isinstance(c, int):
                    at = pl.multiple_of(at, SWEEP)
                for i in slots:
                    total = jnp.zeros((SWEEP, LANES), F32)
                    for j in range(KERNEL):
                        begin = at + (GAP + sign * (j - HALF))
                        total = total + taps_ref[j : j + 1, :] * src[i, pl.ds(begin, SWEEP), :]
                    att[i, pl.ds(at, SWEEP), :] = total
                return 0

            if width <= SWEEP:
                rows_of(0, 0)
            else:
                lax.fori_loop(0, width // SWEEP, rows_of, 0)

        swept(att_pad, 1)
        for i in slots:
            for at in range(0, width, conv_chunk):
                conv = att[i, at : at + conv_chunk, :]
                inv_spread = lax.rsqrt(head_mean(conv * conv, ones_twice) + 1e-05)
                normed = conv * inv_spread
                pre_act = normed * gain
                gate = 1.0 / (1.0 + jnp.exp(-pre_act))
                kept(ox, at, conv_chunk, i, pre_act * gate)
                upper = cx[pl.ds(group[i][0] + at, conv_chunk), :]
                grad_pre = upper * gate * (1.0 + pre_act * (1.0 - gate))
                weighted = grad_pre * gain
                mean = head_mean(weighted * normed, ones_twice)
                grad_conv = (weighted - normed * mean) * inv_spread
                grad_pad[i, GAP + at : GAP + at + conv_chunk, :] = jnp.where(
                    valid[i][at : at + conv_chunk], grad_conv, 0.0
                )
        swept(grad_pad, -1)
        for i in slots:
            att[i, :width, :] = jnp.where(valid[i], att[i, :width, :], 0.0).astype(BF16).astype(F32)

        grads = [att[i, :width, :] * rinv[i, :width, :] for i in slots]
        for i in slots:
            cross = pltpu.roll(-grads[i] * att_pad[i, GAP : GAP + width, :], HEAD_DIM, 1)
            for h in range(heads):
                left = jnp.where(mine[h], grads[i], cross).astype(BF16)
                scores[i, h, :width, :width] = dot_nt(left, v_ones[i][h])
        for i in slots:
            for h in range(heads):
                for at in range(0, width, soft):
                    part = pl.ds(at, soft)
                    ds = weights[i, h, part, :width].astype(F32) * scores[i, h, part, :width]
                    grad_s[i, h, part, :width] = ds.astype(BF16)
        for i in slots:
            outs = [dot_nn(grad_s[i, h, :width, :width], k[i]) for h in range(heads)]
            dq = outs[0] if heads == 1 else jnp.where(low, outs[0], outs[1])
            kept(dqx, 0, width, i, dq * HEAD_DIM ** (-0.5))
            for lhs, rhs, dst in ((q[i], grad_s, dkx), (grads[i], weights, dvx)):
                lhs_t = lhs.T.astype(BF16)
                terms = [
                    dot_nn(lhs_t[h * HEAD_DIM : (h + 1) * HEAD_DIM], rhs[i, h, :width, :width])
                    for h in range(heads)
                ]
                if heads == 1:
                    terms.append(jnp.zeros_like(terms[0]))
                kept(dst, 0, width, i, jnp.concatenate(terms, axis=0).T)

    first = jnp.where(me < half, 0, maxlen)

    longest_near = maxlen - step

    def single(start, length):
        for width in range(step, (longest_near if near else maxlen) + 1, step):

            @pl.when((length <= width) & (length > width - step))
            def _():
                utterances([(base + start, length)], width)

    def double(start, length, other_start, other_length, widths):
        for width in widths:

            @pl.when((length <= width) & (length > width - step))
            def _():
                utterances([(base + start, length), (base + other_start, other_length)], width)

    def visit(i, carry):
        start, head, tail, low_end, high_end, tail_length, head_length, tasks = carry
        length = lengths_ref[i]
        end = start + length
        at_head = (start < 0) & (end > 0)
        at_tail = (start < block) & (end > block)
        at_near = (start >= first) & (end <= first + maxlen) & (length <= longest_near)
        inside = (length > 0) & (start >= 0) & (end <= block) & jnp.logical_not(at_near)

        @pl.when(at_near)
        def _():
            single(start, length)

        short = inside & (length <= 2 * step)
        kind = jnp.where(length > step, 1, 0)
        held = waiting[1, kind]
        both = short & (held > 0)
        task = inside & (both | jnp.logical_not(short))

        @pl.when(task)
        def _():
            noted(tasks, start, length, waiting[0, kind], jnp.where(both, held, 0))

        @pl.when(short)
        def _():
            waiting[0, kind] = start
            waiting[1, kind] = jnp.where(both, 0, length)

        return (
            end,
            jnp.where(at_head, end, head),
            jnp.where(at_tail, start, tail),
            jnp.where(at_near, jnp.minimum(low_end, start), low_end),
            jnp.where(at_near, end, high_end),
            jnp.where(at_tail, length, tail_length),
            jnp.where(at_head, length, head_length),
            tasks + jnp.where(task, 1, 0),
        )

    def noted(at, *numbers):
        for i, number in enumerate(numbers):
            plan_ref[PLAN + 4 * at + i] = number

    if near:
        waiting[1, 0] = 0
        waiting[1, 1] = 0
        carry = (-first_frame, 0, block, block, 0, 0, 0, 0)
        _, *found, tasks = lax.fori_loop(0, utts, visit, carry)
        upper, lower = waiting[1, 1], waiting[1, 0]
        longer = upper > 0
        noted(
            tasks,
            jnp.where(longer, waiting[0, 1], waiting[0, 0]),
            jnp.where(longer, upper, lower),
            waiting[0, 0],
            jnp.where(longer, lower, 0),
        )
        plan_ref[0] = tasks + jnp.where(longer | (lower > 0), 1, 0)
        for i, number in enumerate(found):
            plan_ref[1 + i] = number
    elif not edges:

        def worked(i, _):
            start, length, other, other_length = [plan_ref[PLAN + 4 * i + j] for j in range(4)]

            @pl.when(other_length > 0)
            def _():
                double(start, length, other, other_length, (step, 2 * step))

            @pl.when(other_length == 0)
            def _():
                single(start, length)

            return 0

        lax.fori_loop(0, plan_ref[0], worked, 0)
    if edges:
        head, tail, low_end, high_end, tail_length, head_length = [plan_ref[i] for i in range(1, 7)]
        head_start = head - head_length
        most = jnp.maximum(head_length, tail_length)
        together = (most > maxlen - step) & (jnp.minimum(head_length, tail_length) > maxlen // 2)

        @pl.when(together)
        def _():
            utterances([(base + head_start, head_length), (base + tail, tail_length)], maxlen)

        def one(i, _):
            start = jnp.where(i == 0, head_start, tail)
            length = jnp.where(i == 0, head_length, tail_length)
            single(start, jnp.where(together, 0, length))
            return 0

        lax.fori_loop(0, 2, one, 0)

    frame = lax.broadcasted_iota(jnp.int32, (1, 128), 1)
    for i, src in enumerate((ox, dqx, dkx, dvx)):
        for at in range(0, block, 128):
            tile = src[base + at : base + at + 128, :].T[:channels].astype(BF16)
            if edges:
                crossing = (frame + at < head) | (frame + at >= tail)
                in_near = (frame + at >= low_end) & (frame + at < high_end)
                inner = jnp.where(
                    in_near, before[i][:, at : at + 128], before[4 + i][:, at : at + 128]
                )
                tile = jnp.where(crossing, tile, inner)
            outs[i][:, at : at + 128] = tile


def on_device(queries, keys, values, lengths, conv_weight, norm_gain, cotangent):
    peers, blocks = lax.axis_size("uly"), lax.axis_size("blk")
    piece = queries.shape[0]
    channels = queries.shape[1] // peers
    heads = channels // HEAD_DIM
    block = cotangent.shape[1]
    maxlen = block // 2
    half = peers // 2
    utts = lengths.shape[0]

    smem = pl.BlockSpec(memory_space=pltpu.SMEM)
    vmem = pl.BlockSpec(memory_space=pltpu.VMEM)

    def shaped(count):
        return jax.ShapeDtypeStruct((count, piece, channels), BF16)

    sources = (queries, keys, values)
    if channels % LANES:
        sources = tuple(x.reshape(piece, peers, channels).transpose(1, 0, 2) for x in sources)
    near, far, *parts = pl.pallas_call(
        functools.partial(pack_kernel, (channels, block, maxlen, piece, peers)),
        out_shape=(shaped(maxlen // piece),) * 2 + (shaped(3),) * peers,
        in_specs=[vmem] * 4,
        out_specs=(vmem,) * (2 + peers),
        name="pack",
    )(*sources, cotangent)

    def to_neighbour(x, from_half):
        route = []
        for u in range(peers):
            for b in range(blocks):
                to = b - 1 if (u < half) == (from_half == 0) else b + 1
                if 0 <= to < blocks:
                    route.append((u * blocks + b, u * blocks + to))
        return lax.ppermute(x, ("uly", "blk"), route)

    own = parts[:1] + [None] * (peers - 1)
    order = sorted(range(1, peers), key=lambda d: d)
    for d in order:
        own[d] = lax.ppermute(parts[d], "uly", [(i, i ^ d) for i in range(peers)])
    near_group = jnp.concatenate(own[:half] + [near], axis=0)
    taps, gain = conv_weight, norm_gain[None, :]
    if channels < LANES:
        taps = jnp.pad(taps, ((0, 0), (0, LANES - channels)))
        gain = jnp.pad(gain, ((0, 0), (0, LANES - channels)))
    dims = (heads, block, maxlen, piece, peers, utts, maxlen // 4)
    out = jax.ShapeDtypeStruct((channels, block), BF16)
    plan = jax.ShapeDtypeStruct((PLAN + 4 * (utts + 1),), jnp.int32)

    def call(phase, *arrays):
        rows = block + (2 if phase == "edges" else 1) * maxlen
        held = 32 * rows * LANES + 16 * heads * maxlen * maxlen
        return pl.pallas_call(
            functools.partial(kernel, dims, phase),
            out_shape=(out,) * 4 + (plan,) * (phase == "near"),
            in_specs=[smem] + [vmem] * (len(arrays) - 1),
            out_specs=(vmem,) * 4 + (smem,) * (phase == "near"),
            scratch_shapes=[pltpu.VMEM((rows, LANES), F32)] * 8
            + [pltpu.VMEM((2, heads, maxlen, maxlen), BF16)] * 2
            + [pltpu.VMEM((2, maxlen + 2 * GAP, LANES), F32)] * 2
            + [pltpu.VMEM((2, maxlen, LANES), F32)] * 2
            + [pltpu.VMEM((2, heads, maxlen, maxlen), F32)]
            + [pltpu.SMEM((2, 2), jnp.int32)],
            compiler_params=pltpu.CompilerParams(vmem_limit_bytes=held + 20 * 2**20),
            cost_estimate=pl.CostEstimate(
                flops=24 * heads * block * maxlen * HEAD_DIM,
                bytes_accessed=16 * block * channels,
                transcendentals=heads * block * maxlen,
            ),
            name=phase,
        )(*arrays)

    near_in = to_neighbour(near_group, 0)
    first = call("near", lengths, taps, gain, cotangent, *own[:half])
    own[half], *first, plan = lax.optimization_barrier((own[half], *first))
    far_in = to_neighbour(jnp.concatenate([far] + own[half:], axis=0), 1)

    inner = call("inner", plan, taps, gain, cotangent, *own)
    return call("edges", plan, taps, gain, cotangent, *own, near_in, far_in, *first, *inner)


def solution(mesh):
    in_specs = (
        P(("blk", "uly"), None),
        P(("blk", "uly"), None),
        P(("blk", "uly"), None),
        P(),
        P(None, "uly"),
        P("uly"),
        P("uly", "blk"),
    )
    out_specs = (P("uly", "blk"), P("uly", "blk"), P("uly", "blk"), P("uly", "blk"))
    return jax.shard_map(
        on_device, mesh=mesh, in_specs=in_specs, out_specs=out_specs, check_vma=False
    )
```

```python
import functools

import jax
import jax.numpy as jnp
from jax import lax
from jax.experimental import pallas as pl
from jax.experimental.pallas import tpu as pltpu
from jax.sharding import PartitionSpec as P

KERNEL = 31
HEAD_DIM = 64
HALF = KERNEL // 2
LANES = 128
GAP = 16
PLAN = 8
SWEEP = 128
F32 = jnp.float32
BF16 = jnp.bfloat16


def dot_nt(a, b):
    return lax.dot_general(a, b, (((1,), (1,)), ((), ())), preferred_element_type=F32)


def dot_nn(a, b):
    return lax.dot_general(a, b, (((1,), (0,)), ((), ())), preferred_element_type=F32)


def widened(rows):
    if rows.shape[1] == LANES:
        return rows
    return jnp.concatenate([rows, jnp.zeros_like(rows)], axis=1)


def head_mean(x, ones_twice):
    top = x.astype(BF16)
    rest = (x - top.astype(F32)).astype(BF16)
    return dot_nn(jnp.concatenate([top, rest], axis=1), ones_twice)


def pack_kernel(dims, q_ref, k_ref, v_ref, cot_ref, *outs):
    channels, block, maxlen, piece, peers = dims
    me = lax.axis_index("uly")
    low = me < peers // 2
    near_ref, far_ref = outs[0], outs[1]
    for d in range(peers - 1, -1, -1):
        for i, src in enumerate((q_ref, k_ref, v_ref)):
            if channels % LANES == 0:
                at = pl.ds(pl.multiple_of((me ^ d) * channels, channels), channels)
                tile = src[:, at]
            else:
                tile = src[me ^ d]
            outs[2 + d][i] = tile
    for j in range(maxlen // piece):
        first = cot_ref[:, j * piece : (j + 1) * piece].astype(F32).T.astype(BF16)
        second = cot_ref[:, block - maxlen + j * piece : block - maxlen + (j + 1) * piece]
        second = second.astype(F32).T.astype(BF16)
        near_ref[j] = jnp.where(low, first, second)
        far_ref[j] = jnp.where(low, second, first)


def kernel(dims, phase, lengths_ref, taps_ref, gain_ref, cot_ref, *refs):
    heads, block, maxlen, piece, peers, utts, step = dims
    half = peers // 2
    channels = heads * HEAD_DIM
    near, edges = phase == "near", phase == "edges"
    masked = not edges
    count = half if near else peers
    own_refs, refs = refs[:count], refs[count:]
    if edges:
        (near_in, far_in, *before), refs = refs[:10], refs[10:]
    outs = refs[:4]
    plan_ref = lengths_ref
    if near:
        plan_ref, refs = refs[4], refs[:4] + refs[5:]
    (
        qx, kx, vx, cx, ox, dqx, dkx, dvx, weights, grad_s, att_pad, grad_pad, att, rinv, scores,
        waiting,
    ) = refs[4:]
    me, first_frame = lax.axis_index("uly"), lax.axis_index("blk") * block
    base = maxlen if edges else 0

    def side_row(u, at):
        return pl.multiple_of(jnp.where(u < half, maxlen + block + at, at), piece)

    for d in range(count):
        u = me ^ d
        row = pl.multiple_of(base + u * piece, piece)
        for i, dst in enumerate((qx, kx, vx)):
            dst[pl.ds(row, piece), :] = widened(own_refs[d][i].astype(F32))
        if edges:
            if d < half:
                halo, at = near_in, 3 * d
            else:
                halo, at = far_in, half + 3 * (d - half)
            side = side_row(u, jnp.where(u < half, u, u - half) * piece)
            for i, dst in enumerate((qx, kx, vx)):
                dst[pl.ds(side, piece), :] = widened(halo[at + i].astype(F32))
    for at in range(0, block, 128):
        tile = cot_ref[:, at : at + 128].astype(F32).T
        cx[base + at : base + at + 128, :] = widened(tile)
    if edges:
        for j in range(maxlen // piece):
            for side, src, at in ((me, near_in, 3 * half), (me ^ half, far_in, 0)):
                tile = src[at + j].astype(F32)
                cx[pl.ds(side_row(side, j * piece), piece), :] = widened(tile)
    else:
        for ref in (qx, kx, vx, cx):
            ref[block : block + maxlen, :] = jnp.zeros((maxlen, LANES), F32)
    if near:
        rest = pl.ds(pl.multiple_of(jnp.where(me < half, maxlen, 0), maxlen), maxlen)
        for ref in (qx, kx, vx):
            ref[rest, :] = jnp.zeros((maxlen, LANES), F32)

    lane = lax.broadcasted_iota(jnp.int32, (1, LANES), 1)
    low = lane < HEAD_DIM
    ones_twice = jnp.where(
        lax.broadcasted_iota(jnp.int32, (2 * LANES, LANES), 0) % LANES // HEAD_DIM
        == lax.broadcasted_iota(jnp.int32, (2 * LANES, LANES), 1) // HEAD_DIM,
        1.0 / HEAD_DIM,
        0.0,
    ).astype(BF16)
    gain = gain_ref[...]

    mine = [low, jnp.logical_not(low)][:heads]

    def utterances(group, width):
        slots = range(len(group))
        soft, conv_chunk = min(64, width), 64
        rows = [pl.ds(start, width) for start, _ in group]
        index = lax.broadcasted_iota(jnp.int32, (width, 1), 0)
        column = lax.broadcasted_iota(jnp.int32, (1, width), 1)
        valid = [index < length for _, length in group]
        key_bias = [jnp.where(column < length, 0.0, -1e30) for _, length in group]

        def kept(ref, at, count, slot, new):
            place = pl.ds(group[slot][0] + at, count)
            if masked:
                new = jnp.where(valid[slot][at : at + count], new, ref[place, :])
            ref[place, :] = new

        q, k, v_ones, q_own = [], [], [], []
        for i in slots:
            q.append(qx[rows[i], :] * HEAD_DIM ** (-0.5))
            k.append(kx[rows[i], :].astype(BF16))
            v = vx[rows[i], :]
            v_ones.append([jnp.where(m, v, 1.0).astype(BF16) for m in mine])
            q_own.append([jnp.where(m, q[i], 0.0).astype(BF16) for m in mine])

        for i in slots:
            for h in range(heads):
                scores[i, h, :width, :width] = dot_nt(q_own[i][h], k[i])
        for i in slots:
            for h in range(heads):
                for at in range(0, width, soft):
                    part = pl.ds(at, soft)
                    tile = scores[i, h, part, :width] + key_bias[i]
                    top = jnp.max(tile, axis=1, keepdims=True)
                    weights[i, h, part, :width] = jnp.exp(tile - top).astype(BF16)
        for i in slots:
            accs = [dot_nn(weights[i, h, :width, :width], v_ones[i][h]) for h in range(heads)]
            if heads == 1:
                accs.append(jnp.ones_like(accs[0]))
            total = pltpu.roll(jnp.where(low, accs[1], accs[0]), HEAD_DIM, 1)
            inverse = 1.0 / total
            rinv[i, :width, :] = inverse
            attended = (jnp.where(low, accs[0], accs[1]) * inverse).astype(BF16).astype(F32)
            att_pad[i, GAP : GAP + width, :] = jnp.where(valid[i], attended, 0.0)
            for ref in (att_pad, grad_pad):
                ref[i, :GAP, :] = jnp.zeros((GAP, LANES), F32)
                ref[i, GAP + width : 2 * GAP + width, :] = jnp.zeros((GAP, LANES), F32)

        def swept(src, sign):
            def rows_of(c, _):
                at = c * SWEEP
                if not isinstance(c, int):
                    at = pl.multiple_of(at, SWEEP)
                for i in slots:
                    total = jnp.zeros((SWEEP, LANES), F32)
                    for j in range(KERNEL):
                        begin = at + (GAP + sign * (j - HALF))
                        total = total + taps_ref[j : j + 1, :] * src[i, pl.ds(begin, SWEEP), :]
                    att[i, pl.ds(at, SWEEP), :] = total
                return 0

            if width <= SWEEP:
                rows_of(0, 0)
            else:
                lax.fori_loop(0, width // SWEEP, rows_of, 0)

        swept(att_pad, 1)
        for i in slots:
            for at in range(0, width, conv_chunk):
                conv = att[i, at : at + conv_chunk, :]
                inv_spread = lax.rsqrt(head_mean(conv * conv, ones_twice) + 1e-05)
                normed = conv * inv_spread
                pre_act = normed * gain
                gate = 1.0 / (1.0 + jnp.exp(-pre_act))
                kept(ox, at, conv_chunk, i, pre_act * gate)
                upper = cx[pl.ds(group[i][0] + at, conv_chunk), :]
                grad_pre = upper * gate * (1.0 + pre_act * (1.0 - gate))
                weighted = grad_pre * gain
                mean = head_mean(weighted * normed, ones_twice)
                grad_conv = (weighted - normed * mean) * inv_spread
                grad_pad[i, GAP + at : GAP + at + conv_chunk, :] = jnp.where(
                    valid[i][at : at + conv_chunk], grad_conv, 0.0
                )
        swept(grad_pad, -1)
        for i in slots:
            att[i, :width, :] = jnp.where(valid[i], att[i, :width, :], 0.0).astype(BF16).astype(F32)

        grads = [att[i, :width, :] * rinv[i, :width, :] for i in slots]
        for i in slots:
            cross = pltpu.roll(-grads[i] * att_pad[i, GAP : GAP + width, :], HEAD_DIM, 1)
            for h in range(heads):
                left = jnp.where(mine[h], grads[i], cross).astype(BF16)
                scores[i, h, :width, :width] = dot_nt(left, v_ones[i][h])
        for i in slots:
            for h in range(heads):
                for at in range(0, width, soft):
                    part = pl.ds(at, soft)
                    ds = weights[i, h, part, :width].astype(F32) * scores[i, h, part, :width]
                    grad_s[i, h, part, :width] = ds.astype(BF16)
        for i in slots:
            outs = [dot_nn(grad_s[i, h, :width, :width], k[i]) for h in range(heads)]
            dq = outs[0] if heads == 1 else jnp.where(low, outs[0], outs[1])
            kept(dqx, 0, width, i, dq * HEAD_DIM ** (-0.5))
            for lhs, rhs, dst in ((q[i], grad_s, dkx), (grads[i], weights, dvx)):
                lhs_t = lhs.T.astype(BF16)
                terms = [
                    dot_nn(lhs_t[h * HEAD_DIM : (h + 1) * HEAD_DIM], rhs[i, h, :width, :width])
                    for h in range(heads)
                ]
                if heads == 1:
                    terms.append(jnp.zeros_like(terms[0]))
                kept(dst, 0, width, i, jnp.concatenate(terms, axis=0).T)

    first = jnp.where(me < half, 0, maxlen)

    longest_near = maxlen - step

    def single(start, length):
        for width in range(step, (longest_near if near else maxlen) + 1, step):

            @pl.when((length <= width) & (length > width - step))
            def _():
                utterances([(base + start, length)], width)

    def double(start, length, other_start, other_length, widths):
        for width in widths:

            @pl.when((length <= width) & (length > width - step))
            def _():
                utterances([(base + start, length), (base + other_start, other_length)], width)

    def visit(i, carry):
        start, head, tail, low_end, high_end, tail_length, head_length, tasks, closed = carry
        length = lengths_ref[i]
        end = start + length
        at_head = (start < 0) & (end > 0)
        at_tail = (start < block) & (end > block)
        in_half = (start >= first) & (end <= first + maxlen)
        closed = jnp.where(in_half & (length > longest_near), 1, closed)
        at_near = in_half & (closed == 0)
        inside = (length > 0) & (start >= 0) & (end <= block) & jnp.logical_not(at_near)

        @pl.when(at_near)
        def _():
            single(start, length)

        short = inside & (length <= 2 * step)
        kind = jnp.where(length > step, 1, 0)
        held = waiting[1, kind]
        both = short & (held > 0)
        task = inside & (both | jnp.logical_not(short))

        @pl.when(task)
        def _():
            noted(tasks, start, length, waiting[0, kind], jnp.where(both, held, 0))

        @pl.when(short)
        def _():
            waiting[0, kind] = start
            waiting[1, kind] = jnp.where(both, 0, length)

        return (
            end,
            jnp.where(at_head, end, head),
            jnp.where(at_tail, start, tail),
            jnp.where(at_near, jnp.minimum(low_end, start), low_end),
            jnp.where(at_near, end, high_end),
            jnp.where(at_tail, length, tail_length),
            jnp.where(at_head, length, head_length),
            tasks + jnp.where(task, 1, 0),
            closed,
        )

    def noted(at, *numbers):
        for i, number in enumerate(numbers):
            plan_ref[PLAN + 4 * at + i] = number

    if near:
        waiting[1, 0] = 0
        waiting[1, 1] = 0
        carry = (-first_frame, 0, block, block, 0, 0, 0, 0, 0)
        _, *found, tasks, _ = lax.fori_loop(0, utts, visit, carry)
        upper, lower = waiting[1, 1], waiting[1, 0]
        longer = upper > 0
        noted(
            tasks,
            jnp.where(longer, waiting[0, 1], waiting[0, 0]),
            jnp.where(longer, upper, lower),
            waiting[0, 0],
            jnp.where(longer, lower, 0),
        )
        plan_ref[0] = tasks + jnp.where(longer | (lower > 0), 1, 0)
        for i, number in enumerate(found):
            plan_ref[1 + i] = number
    elif not edges:

        def worked(i, _):
            start, length, other, other_length = [plan_ref[PLAN + 4 * i + j] for j in range(4)]

            @pl.when(other_length > 0)
            def _():
                double(start, length, other, other_length, (step, 2 * step))

            @pl.when(other_length == 0)
            def _():
                single(start, length)

            return 0

        lax.fori_loop(0, plan_ref[0], worked, 0)
    if edges:
        head, tail, low_end, high_end, tail_length, head_length = [plan_ref[i] for i in range(1, 7)]
        head_start = head - head_length
        most = jnp.maximum(head_length, tail_length)
        together = (most > maxlen - step) & (jnp.minimum(head_length, tail_length) > maxlen // 2)

        @pl.when(together)
        def _():
            utterances([(base + head_start, head_length), (base + tail, tail_length)], maxlen)

        def one(i, _):
            start = jnp.where(i == 0, head_start, tail)
            length = jnp.where(i == 0, head_length, tail_length)
            single(start, jnp.where(together, 0, length))
            return 0

        lax.fori_loop(0, 2, one, 0)

    frame = lax.broadcasted_iota(jnp.int32, (1, 128), 1)
    for i, src in enumerate((ox, dqx, dkx, dvx)):
        for at in range(0, block, 128):
            tile = src[base + at : base + at + 128, :].T[:channels].astype(BF16)
            if edges:
                crossing = (frame + at < head) | (frame + at >= tail)
                in_near = (frame + at >= low_end) & (frame + at < high_end)
                inner = jnp.where(
                    in_near, before[i][:, at : at + 128], before[4 + i][:, at : at + 128]
                )
                tile = jnp.where(crossing, tile, inner)
            outs[i][:, at : at + 128] = tile


def on_device(queries, keys, values, lengths, conv_weight, norm_gain, cotangent):
    peers, blocks = lax.axis_size("uly"), lax.axis_size("blk")
    piece = queries.shape[0]
    channels = queries.shape[1] // peers
    heads = channels // HEAD_DIM
    block = cotangent.shape[1]
    maxlen = block // 2
    half = peers // 2
    utts = lengths.shape[0]

    smem = pl.BlockSpec(memory_space=pltpu.SMEM)
    vmem = pl.BlockSpec(memory_space=pltpu.VMEM)

    def shaped(count):
        return jax.ShapeDtypeStruct((count, piece, channels), BF16)

    sources = (queries, keys, values)
    if channels % LANES:
        sources = tuple(x.reshape(piece, peers, channels).transpose(1, 0, 2) for x in sources)
    near, far, *parts = pl.pallas_call(
        functools.partial(pack_kernel, (channels, block, maxlen, piece, peers)),
        out_shape=(shaped(maxlen // piece),) * 2 + (shaped(3),) * peers,
        in_specs=[vmem] * 4,
        out_specs=(vmem,) * (2 + peers),
        name="pack",
    )(*sources, cotangent)

    def to_neighbour(x, from_half):
        route = []
        for u in range(peers):
            for b in range(blocks):
                to = b - 1 if (u < half) == (from_half == 0) else b + 1
                if 0 <= to < blocks:
                    route.append((u * blocks + b, u * blocks + to))
        return lax.ppermute(x, ("uly", "blk"), route)

    own = parts[:1] + [None] * (peers - 1)
    order = sorted(range(1, peers), key=lambda d: d)
    for d in order:
        own[d] = lax.ppermute(parts[d], "uly", [(i, i ^ d) for i in range(peers)])
    near_group = jnp.concatenate(own[:half] + [near], axis=0)
    taps, gain = conv_weight, norm_gain[None, :]
    if channels < LANES:
        taps = jnp.pad(taps, ((0, 0), (0, LANES - channels)))
        gain = jnp.pad(gain, ((0, 0), (0, LANES - channels)))
    dims = (heads, block, maxlen, piece, peers, utts, maxlen // 4)
    out = jax.ShapeDtypeStruct((channels, block), BF16)
    plan = jax.ShapeDtypeStruct((PLAN + 4 * (utts + 1),), jnp.int32)

    def call(phase, *arrays):
        rows = block + (2 if phase == "edges" else 1) * maxlen
        held = 32 * rows * LANES + 16 * heads * maxlen * maxlen
        return pl.pallas_call(
            functools.partial(kernel, dims, phase),
            out_shape=(out,) * 4 + (plan,) * (phase == "near"),
            in_specs=[smem] + [vmem] * (len(arrays) - 1),
            out_specs=(vmem,) * 4 + (smem,) * (phase == "near"),
            scratch_shapes=[pltpu.VMEM((rows, LANES), F32)] * 8
            + [pltpu.VMEM((2, heads, maxlen, maxlen), BF16)] * 2
            + [pltpu.VMEM((2, maxlen + 2 * GAP, LANES), F32)] * 2
            + [pltpu.VMEM((2, maxlen, LANES), F32)] * 2
            + [pltpu.VMEM((2, heads, maxlen, maxlen), F32)]
            + [pltpu.SMEM((2, 2), jnp.int32)],
            compiler_params=pltpu.CompilerParams(vmem_limit_bytes=held + 20 * 2**20),
            cost_estimate=pl.CostEstimate(
                flops=24 * heads * block * maxlen * HEAD_DIM,
                bytes_accessed=16 * block * channels,
                transcendentals=heads * block * maxlen,
            ),
            name=phase,
        )(*arrays)

    near_in = to_neighbour(near_group, 0)
    first = call("near", lengths, taps, gain, cotangent, *own[:half])
    own[half], *first, plan = lax.optimization_barrier((own[half], *first))
    far_in = to_neighbour(jnp.concatenate([far] + own[half:], axis=0), 1)

    inner = call("inner", plan, taps, gain, cotangent, *own)
    return call("edges", plan, taps, gain, cotangent, *own, near_in, far_in, *first, *inner)


def solution(mesh):
    in_specs = (
        P(("blk", "uly"), None),
        P(("blk", "uly"), None),
        P(("blk", "uly"), None),
        P(),
        P(None, "uly"),
        P("uly"),
        P("uly", "blk"),
    )
    out_specs = (P("uly", "blk"), P("uly", "blk"), P("uly", "blk"), P("uly", "blk"))
    return jax.shard_map(
        on_device, mesh=mesh, in_specs=in_specs, out_specs=out_specs, check_vma=False
    )
```
